512 devices in a mesh: ctx: 256 (over z, x, y_lo, core), head: 2 (over y_hi).
Axes of the slice: x: 4, y: 4 (y_hi: 2, y_lo: 2; y = y_hi * 2 + y_lo), z: 16, core: 2. Of those that a mesh axis runs over, the one named last changes fastest.
Arguments:
- q_nope: bfloat16 [65536, 16, 128], P('ctx', 'head'), may hold values from -6 to 6
- q_rope: bfloat16 [65536, 16, 64], P('ctx', 'head'), may hold values from -300 to 300
- c_kv: bfloat16 [65536, 512], P('ctx'), may hold values from -6 to 6
- k_rope: bfloat16 [65536, 64], P('ctx'), may hold values from -6 to 6
- block_pos: int32 [512], replicated, may hold values from 0 to 511, as said below
- w_uk: bfloat16 [16, 128, 512], P('head'), may hold values from -0.5 to 0.5
- w_uv: bfloat16 [16, 512, 128], P('head'), may hold values from -6 to 6
Outputs:
- attn_out: bfloat16 [65536, 16, 128], P('ctx', 'head')
The draws below stay inside these ranges and needn't reach their ends.
Inputs may be any that keep to these rules, and one draw needn't show every extreme that they name: block_pos is the mirrored-pair order turned by some c: block_pos[2 s] = (s + c) mod 256 and block_pos[2 s + 1] = 511 - block_pos[2 s].
All inputs are finite; a program needn't handle non-finite values.
Results may differ from the reference program's by a relative error of at most 0.0072.
Values may be sent and summed in bfloat16 or wider, within the bound.
No kernel may reach another device: no remote copies, remote signals or barrier semaphores. Data moves between devices by JAX's collectives and lax.ppermute only.
A program may use at most 64 MiB of HBM per device.

```python
import math
import jax
import jax.numpy as jnp
from jax import lax

LAT = 512
ROPE = 64
NOPE = 128
VDIM = 128
H = 16
BLK = 128
TOKENS = 65536
N_CTX = 256


def rope_pair(key, strength):
    base_k = jnp.clip(jax.random.normal(jax.random.fold_in(key, 101), (TOKENS, ROPE), jnp.float32), -5.0, 5.0)
    base_q = jnp.clip(jax.random.normal(jax.random.fold_in(key, 102), (TOKENS, H, ROPE), jnp.float32), -5.0, 5.0)
    row_ids = jnp.arange(TOKENS)
    active = strength > 0
    leader = (row_ids % 16 == 9) & active
    trailer = (row_ids % 16 == 8) & active
    keys = jnp.where(trailer[:, None], jnp.roll(base_k, -1, axis=0) * 1.012, base_k)
    factor = strength * (1.0 + 0.6 * (jnp.arange(H) % 3).astype(jnp.float32))
    queries = jnp.where(leader[:, None, None], factor[None, :, None] * keys[:, None, :], base_q)
    return (queries, keys)


def draw_q_rope(key, part):
    strength = 0.0
    queries, keys = rope_pair(key, strength)
    return queries.astype(jnp.bfloat16)


def draw_k_rope(key, part):
    strength = 0.0
    queries, keys = rope_pair(key, strength)
    return keys.astype(jnp.bfloat16)


def draw_block_pos(key, part):
    key = jax.random.fold_in(key, 7)
    turn = jax.random.randint(key, (), 0, N_CTX, dtype=jnp.int32)
    first = (jnp.arange(N_CTX, dtype=jnp.int32) + turn) % N_CTX
    second = 2 * N_CTX - 1 - first
    return jnp.stack([first, second], axis=1).reshape(-1).astype(jnp.int32)


def shard_levels(key, shape, shards, smallest, top_value):
    loudness, own = 1.0, jax.random.fold_in(key, 6)
    for axis_at, parts in shards:
        heights = jnp.exp(jax.random.uniform(jax.random.fold_in(own, axis_at), (parts,), jnp.float32, smallest / len(shards), top_value / len(shards)))
        loudness = loudness * jnp.repeat(heights, shape[axis_at] // parts).reshape([-1 if axis == axis_at else 1 for axis in range(len(shape))])
    return loudness


def bell_draw(rng, dims, width, limit, shards=(), held_as=jnp.bfloat16):
    level = shard_levels(rng, dims, shards, -0.22, 0.18) if shards else 1.0
    entries = jax.random.normal(rng, dims, jnp.float32) * width * level
    return jnp.minimum(jnp.maximum(entries, -limit), limit).astype(held_as)


def setup_inputs(seed: int = 0) -> dict:
    key_of = jax.random.split(jax.random.key(seed), 8)
    return {
        "q_nope": bell_draw(key_of[0], (TOKENS, H, NOPE), 1.0, 6.0, ((0, 256), (1, 2))),
        "q_rope": draw_q_rope(jax.random.fold_in(key_of[7], 71), 0),
        "c_kv": bell_draw(key_of[2], (TOKENS, LAT), 1.0, 6.0, ((0, 256),)),
        "k_rope": draw_k_rope(jax.random.fold_in(key_of[7], 71), 0),
        "block_pos": draw_block_pos(jax.random.fold_in(key_of[7], 71), 0),
        "w_uk": bell_draw(key_of[5], (H, NOPE, LAT), NOPE ** -0.5, 0.5, ((0, 2),)),
        "w_uv": bell_draw(key_of[6], (H, LAT, VDIM), 1.0, 6.0, ((0, 2),)),
    }


def reference(q_nope, q_rope, c_kv, k_rope, block_pos, w_uk, w_uv):
    rows = 2 * BLK
    scale = 1.0 / math.sqrt(NOPE + ROPE)
    span = jnp.arange(BLK, dtype=jnp.int32)
    uk_full = w_uk.astype(jnp.float32)
    uv_full = w_uv.astype(jnp.float32)

    def positions(source):
        pair = lax.dynamic_slice_in_dim(block_pos, (2 * source).astype(jnp.int32), 2)
        return (pair[:, None] * BLK + span[None, :]).reshape(-1)

    def one_shard(place):
        start = (place * rows).astype(jnp.int32)
        nope_rows = lax.dynamic_slice_in_dim(q_nope, start, rows, 0).astype(jnp.float32)
        rope_rows = lax.dynamic_slice_in_dim(q_rope, start, rows, 0).astype(jnp.float32)
        q_lat = jnp.einsum('thn,hnl->thl', nope_rows, uk_full).astype(jnp.bfloat16)
        q_lat = lax.optimization_barrier(q_lat).astype(jnp.float32)
        latents = []
        ropes = []
        key_pos = []
        for offset in (0, 1, -1, 2, -2):
            source = ((place - offset) % N_CTX).astype(jnp.int32)
            first = (source * rows).astype(jnp.int32)
            latents.append(lax.dynamic_slice_in_dim(c_kv, first, rows, 0))
            ropes.append(lax.dynamic_slice_in_dim(k_rope, first, rows, 0))
            key_pos.append(positions(source))
        latent = jnp.concatenate(latents, axis=0).astype(jnp.float32)
        rotary = jnp.concatenate(ropes, axis=0).astype(jnp.float32)
        kpos = jnp.concatenate(key_pos, axis=0)
        qpos = positions(place.astype(jnp.int32))
        score = (jnp.einsum('thl,kl->thk', q_lat, latent) + jnp.einsum('thr,kr->thk', rope_rows, rotary)) * scale
        visible = kpos[None, None, :] <= qpos[:, None, None]
        score = jnp.where(visible, score, -1e+30)
        top = lax.optimization_barrier(jnp.max(score, axis=2, keepdims=True))
        expo = jnp.where(visible, jnp.exp(score - top), 0.0)
        total = lax.optimization_barrier(jnp.sum(expo, axis=2))
        weights = lax.optimization_barrier(expo.astype(jnp.bfloat16)).astype(jnp.float32)
        o_lat = jnp.einsum('thk,kl->thl', weights, latent) / total[:, :, None]
        o_lat = lax.optimization_barrier(o_lat.astype(jnp.bfloat16)).astype(jnp.float32)
        return jnp.einsum('thl,hlv->thv', o_lat, uv_full).astype(jnp.bfloat16)
    blocks = lax.map(one_shard, jnp.arange(N_CTX, dtype=jnp.int32))
    return blocks.reshape(TOKENS, H, VDIM)
```

```python
import math
import functools
import jax
import jax.numpy as jnp
from jax import lax
from jax.experimental import pallas as pl
from jax.experimental.pallas import tpu as pltpu
from jax.sharding import PartitionSpec as P

NEG = -1e30
LOG2E = 1.4426950408889634


def blocks_kernel(offsets, mchunk, *refs):
    ns = len(refs) - 15
    pos, qn, qr, wk, wv = refs[:5]
    shards = refs[5:5 + ns]
    out = refs[5 + ns]
    qf, qs, kt, vs, ss, os_, low_l, high_l, of = refs[6 + ns:]
    T, H, N = qn.shape
    B = T // 2
    LATW = wk.shape[2]
    R = qr.shape[1]
    W = qs.shape[2]
    HB = H * B
    c2 = LOG2E / math.sqrt(N + R)
    place = lax.axis_index("ctx")
    nctx = pos.shape[0] // 2

    def a_of(off):
        return pos[2 * lax.rem(place - off + nctx, nctx)]

    mine = a_of(0)
    nl = jnp.int32(0)
    nh = jnp.int32(0)
    for i, off in enumerate(offsets(place)):
        if i == 0:
            low_l[nl] = 0
            high_l[nh] = 0
            high_l[nh + 1] = 1
            nl, nh = nl + 1, nh + 2
        else:
            lt = (a_of(off) < mine).astype(jnp.int32)
            low_l[nl] = 2 * i
            nl = nl + lt
            high_l[nh] = 2 * i
            high_l[nh + 1] = 2 * i + 1
            nh = nh + 2 - lt
    low_l[nl] = 0
    high_l[nh] = 0

    zero_k = jnp.zeros((W - LATW - R, B), jnp.bfloat16)
    for i, sh in enumerate(shards):
        rope = sh[T:, :]
        rope = jnp.concatenate([rope[:, :T], rope[:, T:]], axis=0)
        for b in range(2):
            c = sh[b * B:(b + 1) * B, :]
            vs[2 * i + b] = c
            kt[2 * i + b, :LATW, :] = c.T
            kt[2 * i + b, LATW:LATW + R, :] = rope[:, b * B:(b + 1) * B]
            kt[2 * i + b, LATW + R:, :] = zero_k

    qf[...] = qn[...].astype(jnp.float32).reshape(T * H, N)
    zero_q = jnp.zeros((B, W - LATW - R), jnp.bfloat16)
    for h in range(H):
        q = qf[pl.ds(h, T, stride=H), :].astype(jnp.bfloat16)
        ql = jnp.dot(q, wk[h], preferred_element_type=jnp.float32).astype(jnp.bfloat16)
        qrt = qr[h].T
        for b in range(2):
            rr = slice(h * B, (h + 1) * B)
            qs[b, rr, :LATW] = ql[b * B:(b + 1) * B]
            qs[b, rr, LATW:LATW + R] = qrt[b * B:(b + 1) * B]
            qs[b, rr, LATW + R:] = zero_q

    def process(half, n, lst, nb):
        MC = mchunk
        k_items = []
        v_items = []
        for i in range(n):
            b0, b1 = lst[2 * i], lst[2 * i + 1]
            k_items.append(jnp.concatenate([kt[b0], kt[b1]], axis=1))
            v_items.append(jnp.concatenate([vs[b0], vs[b1]], axis=0))
        even = nb == 2 * n
        for i in range(n):
            s = jnp.dot(qs[half], k_items[i], preferred_element_type=jnp.float32)
            if i == 0:
                t_id = lax.broadcasted_iota(jnp.int32, (HB, B), 0) % B
                k_id = lax.broadcasted_iota(jnp.int32, (HB, B), 1)
                tri = k_id <= t_id
                if half == 0:
                    s = jnp.concatenate([jnp.where(tri, s[:, :B], NEG), s[:, B:]], axis=1)
                else:
                    s = jnp.concatenate([s[:, :B], jnp.where(tri, s[:, B:], NEG)], axis=1)
            if i == n - 1:
                s = jnp.concatenate([s[:, :B], jnp.where(even, s[:, B:], NEG)], axis=1)
            ss[:, i * 2 * B:(i + 1) * 2 * B] = s
        for r in range(HB // MC):
            rr = slice(r * MC, (r + 1) * MC)
            mx = ss[rr, :B]
            for j in range(1, 2 * n):
                mx = jnp.maximum(mx, ss[rr, j * B:(j + 1) * B])
            m = jnp.max(mx, axis=1, keepdims=True)
            ps = []
            l = jnp.zeros((MC, B), jnp.float32)
            for j in range(2 * n):
                p = jnp.exp2((ss[rr, j * B:(j + 1) * B] - m) * c2)
                l = l + p
                ps.append(p.astype(jnp.bfloat16))
            tot = jnp.sum(l, axis=1, keepdims=True)
            o = jnp.dot(jnp.concatenate(ps, axis=1), jnp.concatenate(v_items, axis=0), preferred_element_type=jnp.float32)
            os_[half, rr, :] = (o / tot).astype(jnp.bfloat16)

    for half, lst, nb in ((0, low_l, nl), (1, high_l, nh)):
        items = (nb + 1) // 2
        for n in range(1, 6):
            if half == 0 and n > 3 or half == 1 and n < 3:
                continue
            @pl.when(items == n)
            def _(half=half, n=n, lst=lst, nb=nb):
                process(half, n, lst, nb)

    for h in range(H):
        o = jnp.concatenate([os_[0, h * B:(h + 1) * B, :], os_[1, h * B:(h + 1) * B, :]], axis=0)
        of[pl.ds(h, T, stride=H), :] = jnp.dot(o, wv[h], preferred_element_type=jnp.float32)
    out[...] = of[...].reshape(T, H, N).astype(jnp.bfloat16)


def attend(pos, qn, qrt, wk, wv, shards, offsets, mchunk=256):
    T, H, N = qn.shape
    B = T // 2
    ns = len(shards)
    R = qrt.shape[1]
    W = 640
    vm = pl.BlockSpec(memory_space=pltpu.VMEM)
    return pl.pallas_call(
        functools.partial(blocks_kernel, offsets, mchunk),
        out_shape=jax.ShapeDtypeStruct((T, H, N), jnp.bfloat16),
        in_specs=[pl.BlockSpec(memory_space=pltpu.SMEM)] + [vm] * (4 + ns),
        out_specs=vm,
        scratch_shapes=[
            pltpu.VMEM((T * H, N), jnp.float32),
            pltpu.VMEM((2, H * B, W), jnp.bfloat16),
            pltpu.VMEM((2 * ns, W, B), jnp.bfloat16),
            pltpu.VMEM((2 * ns, B, 512), jnp.bfloat16),
            pltpu.VMEM((H * B, 10 * B), jnp.float32),
            pltpu.VMEM((2, H * B, 512), jnp.bfloat16),
            pltpu.SMEM((16,), jnp.int32),
            pltpu.SMEM((16,), jnp.int32),
            pltpu.VMEM((T * H, N), jnp.float32),
        ],
        compiler_params=pltpu.CompilerParams(vmem_limit_bytes=28 * 1024 * 1024),
        name="attend",
    )(pos, qn, qrt, wk, wv, *shards)


def pack_kernel(c, r, out):
    rows = c.shape[0]
    half = r.shape[0] // 2
    out[:rows, :] = c[...]
    out[rows:, :rows] = r[:half, :]
    out[rows:, rows:] = r[half:, :]


def pack(c_kv, k_rope_t):
    rows, width = c_kv.shape
    vm = pl.BlockSpec(memory_space=pltpu.VMEM)
    return pl.pallas_call(
        pack_kernel,
        out_shape=jax.ShapeDtypeStruct((rows + k_rope_t.shape[0] // 2, width), c_kv.dtype),
        in_specs=[vm, vm],
        out_specs=vm,
        name="pack",
    )(c_kv, k_rope_t)


def pairs(n, heads, source):
    out = []
    for t in range(n):
        s = source(t) % n
        for h in range(heads):
            hs = h if s // 4 == t // 4 else heads - 1 - h
            out.append((s * heads + hs, t * heads + h))
    return out


def per_device(q_nope, q_rope, c_kv, k_rope, block_pos, w_uk, w_uv):
    n, heads = lax.axis_size("ctx"), lax.axis_size("head")
    send = lambda x, source: lax.ppermute(x, ("ctx", "head"), pairs(n, heads, source))
    mine = pack(c_kv, k_rope.T)
    mate = send(mine, lambda t: t ^ 1)
    cross = send(mine, lambda t: t - 1 if t % 2 == 0 else t + 1)
    above = send(mine, lambda t: t + 2)
    below = send(mine, lambda t: t - 2)
    q_rope_t = jnp.transpose(q_rope, (1, 2, 0))

    def offsets(place):
        odd = lax.rem(place, 2)
        return (0, 2 * odd - 1, 1 - 2 * odd, 2, -2)

    return attend(block_pos, q_nope, q_rope_t, w_uk, w_uv, (mine, mate, cross, below, above), offsets)


def solution(mesh):
    placed = (
        P("ctx", "head", None),
        P("ctx", "head", None),
        P("ctx", None),
        P("ctx", None),
        P(),
        P("head", None, None),
        P("head", None, None),
    )
    return jax.shard_map(
        per_device, mesh=mesh, in_specs=placed, out_specs=P("ctx", "head", None), check_vma=False
    )
```

```python
import functools
import math

import jax
import jax.numpy as jnp
from jax import lax
from jax.experimental import pallas as pl
from jax.experimental.pallas import tpu as pltpu
from jax.sharding import PartitionSpec as P

NEG = -1e30
LOG2E = 1.4426950408889634
CHUNK = 256
AHEAD = 3
MIB = 1024 * 1024
FL = 4e9


def place_now():
    return lax.axis_index("ctx")


def phase_kernel(first, last, offsets, ns, split, when, again, *refs):
    refs = list(refs)
    take = lambda k: [refs.pop(0) for _ in range(k)]
    (pos,) = take(1)
    if first:
        qn_h, qr_h, wk_h = take(3)
    else:
        qs, m_in, l_in, o_in = take(4)
    if last:
        (wv_h,) = take(1)
    shards = [take(2) if i in split else take(1)[0] for i in range(ns)]
    if first and again:
        take(4)
    if last:
        (out_h,) = take(1)
        if first:
            (qs,) = take(1)
    else:
        if first:
            (qs,) = take(1)
        m_out, l_out, o_out = take(3)
        if first and not again:
            (passed,) = take(1)
            passed[...] = shards[0][...]
    kt, vs, low_l, high_l = take(4)
    copies = []
    if first:
        qn, qr, wk, qf, sem_q = take(5)
        copies = [
            pltpu.make_async_copy(qn_h, qn, sem_q.at[0]),
            pltpu.make_async_copy(wk_h, wk, sem_q.at[1]),
            pltpu.make_async_copy(qr_h, qr, sem_q.at[2]),
        ]
    if last:
        wv, os_, of, ob, sem_w, sem_o = take(6)
        copy_w = pltpu.make_async_copy(wv_h, wv, sem_w)
    def run():
        for copy in copies:
            copy.start()
        if last:
            copy_w.start()

        _, HB, W = qs.shape
        B = kt.shape[2]
        LATW = vs.shape[2]
        T = 2 * B
        H = HB // B
        R = 2 * (shards[0].shape[0] - T)
        c2 = LOG2E / math.sqrt(LATW // 4 + R)
        place = place_now()
        nctx = pos.shape[0] // 2

        def a_of(off):
            return pos[2 * lax.rem(place - off + nctx, nctx)]

        mine = a_of(0)
        nl = jnp.int32(0)
        nh = jnp.int32(0)
        for i, off in enumerate(offsets(place)):
            if first and i == 0:
                low_l[nl] = 0
                high_l[nh] = 0
                high_l[nh + 1] = 1
                nl, nh = nl + 1, nh + 2
            else:
                lt = (a_of(off) < mine).astype(jnp.int32)
                low_l[nl] = 2 * i
                nl = nl + lt
                high_l[nh] = 2 * i
                high_l[nh + 1] = 2 * i + 1
                nh = nh + 2 - lt
        low_l[nl] = 0
        high_l[nh] = 0

        zero_k = jnp.zeros((W - LATW - R, B), jnp.bfloat16)
        def ready(i, sh):
            rope = sh[T:, :]
            rope = jnp.concatenate([rope[:, :T], rope[:, T:]], axis=0)
            for b in range(2):
                c = sh[b * B:(b + 1) * B, :]
                vs[2 * i + b] = c
                kt[2 * i + b, :LATW, :] = c.T
                kt[2 * i + b, LATW:LATW + R, :] = rope[:, b * B:(b + 1) * B]
                kt[2 * i + b, LATW + R:, :] = zero_k

        for i, sh in enumerate(shards):
            if i in split:
                for odd in range(2):
                    pl.when(lax.rem(place, 2) == odd)(functools.partial(ready, i, sh[odd]))
            else:
                ready(i, sh)

        if first:
            N = wk.shape[1]
            copies[0].wait()
            qf[...] = qn[...].astype(jnp.float32).reshape(T * H, N)
            zero_q = jnp.zeros((B, W - LATW - R), jnp.bfloat16)
            copies[1].wait()
            copies[2].wait()
            for h in range(H):
                q = qf[pl.ds(h, T, stride=H), :].astype(jnp.bfloat16)
                ql = jnp.dot(q, wk[h], preferred_element_type=jnp.float32).astype(jnp.bfloat16)
                qrt = qr[h].T
                for b in range(2):
                    rr = slice(h * B, (h + 1) * B)
                    qs[b, rr, :LATW] = ql[b * B:(b + 1) * B]
                    qs[b, rr, LATW:LATW + R] = qrt[b * B:(b + 1) * B]
                    qs[b, rr, LATW + R:] = zero_q

        def process(*jobs):
            rows = []
            for half, n, lst, nb in jobs:
                k_items = []
                v_items = []
                for i in range(n):
                    b0, b1 = lst[2 * i], lst[2 * i + 1]
                    k_items.append(jnp.concatenate([kt[b0], kt[b1]], axis=1))
                    v_items.append(jnp.concatenate([vs[b0], vs[b1]], axis=0))
                for r in range(HB // CHUNK):
                    rows.append((half, slice(r * CHUNK, (r + 1) * CHUNK), n, nb, k_items, v_items))

            def scores(half, rr, n, nb, k_items, v_items):
                parts = []
                q = qs[half, rr, :]
                for i in range(n):
                    s = jnp.dot(q, k_items[i], preferred_element_type=jnp.float32)
                    s0, s1 = s[:, :B], s[:, B:]
                    if first and i == 0:
                        t_id = lax.broadcasted_iota(jnp.int32, (CHUNK, B), 0) % B
                        k_id = lax.broadcasted_iota(jnp.int32, (CHUNK, B), 1)
                        if half == 0:
                            s0 = jnp.where(k_id <= t_id, s0, NEG)
                        else:
                            s1 = jnp.where(k_id <= t_id, s1, NEG)
                    if nb is not None and i == n - 1:
                        s1 = jnp.where(nb == 2 * n, s1, NEG)
                    parts += [s0, s1]
                return parts

            def weigh(part, half, rr, n, nb, k_items, v_items):
                if n == 0:
                    return m_in[half, rr, :1], l_in[half, rr, :], o_in[half, rr, :]
                mx = part[0]
                for j in range(1, 2 * n):
                    mx = jnp.maximum(mx, part[j])
                m = jnp.max(mx, axis=1, keepdims=True)
                if first:
                    l = jnp.zeros((CHUNK, B), jnp.float32)
                else:
                    old = m_in[half, rr, :1]
                    m = jnp.maximum(m, old)
                    alpha = jnp.exp2((old - m) * c2)
                    l = l_in[half, rr, :] * alpha
                ps = []
                for j in range(2 * n):
                    p = jnp.exp2((part[j] - m) * c2)
                    l = l + p
                    ps.append(p.astype(jnp.bfloat16))
                o = jnp.dot(
                    jnp.concatenate(ps, axis=1), jnp.concatenate(v_items, axis=0), preferred_element_type=jnp.float32
                )
                if not first:
                    o = o + o_in[half, rr, :] * alpha
                return m, l, o

            def keep(half, rr, m, l, o):
                if last:
                    inv = 1.0 / jnp.sum(l, axis=1, keepdims=True)
                    os_[half, rr, :] = (o * inv).astype(jnp.bfloat16)
                else:
                    m_out[half, rr, :] = jnp.broadcast_to(m, (CHUNK, B))
                    l_out[half, rr, :] = l
                    o_out[half, rr, :] = o

            waiting = [scores(*row) for row in rows[:AHEAD]]
            for r, row in enumerate(rows):
                if r + AHEAD < len(rows):
                    waiting.append(scores(*rows[r + AHEAD]))
                keep(*row[:2], *weigh(waiting[r], *row))
                if last and (r + 1 == len(rows) or rows[r + 1][0] != row[0]):
                    output(row[0])

        def output(half):
            if half == 0:
                copy_w.wait()
            for h in range(H):
                o = os_[half, h * B:(h + 1) * B, :]
                of[pl.ds(half * HB + h, B, stride=H), :] = jnp.dot(o, wv[h], preferred_element_type=jnp.float32)
            rows = slice(half * HB, (half + 1) * HB)
            ob[half * B:(half + 1) * B] = of[rows, :].reshape(B, H, of.shape[1]).astype(jnp.bfloat16)
            out_copy(half).start()

        def out_copy(half):
            return pltpu.make_async_copy(ob.at[pl.ds(half * B, B)], out_h.at[pl.ds(half * B, B)], sem_o.at[half])

        if first:
            counts = [((2 + j) // 2, (2 * ns - j + 1) // 2) for j in range(ns)]
        else:
            counts = [((j + 1) // 2, (2 * ns - j + 1) // 2) for j in range(ns + 1)]
        if len(counts) == 1:
            process((0, counts[0][0], low_l, nl), (1, counts[0][1], high_l, nh))
        elif ns == 4:
            usual = nl == 2
            pl.when(usual)(lambda: process((0, *counts[2][:1], low_l, None), (1, counts[2][1], high_l, None)))
            for half, lst, nb in ((0, low_l, nl), (1, high_l, nh)):
                items = (nb + 1) // 2
                for n in sorted({c[half] for j, c in enumerate(counts) if j != 2}):
                    pl.when((items == n) & (nl != 2))(functools.partial(process, (half, n, lst, nb)))
        else:
            for half, lst, nb in ((0, low_l, nl), (1, high_l, nh)):
                items = (nb + 1) // 2
                for n in sorted({c[half] for c in counts}):
                    pl.when(items == n)(functools.partial(process, (half, n, lst, nb)))
        if last:
            for half in range(2):
                out_copy(half).wait()

    if when is None:
        run()
    else:
        pl.when(when(place_now()))(run)


def phase(first, last, offsets, pos, queries, w_uv, shards, when=None, state=None, limit=14):
    ns = len(shards)
    split = [i for i, sh in enumerate(shards) if isinstance(sh, tuple)]
    shards = [x for sh in shards for x in (sh if isinstance(sh, tuple) else (sh,))]
    T = 256
    B = T // 2
    LATW = shards[0].shape[1]
    R = 2 * (shards[0].shape[0] - T)
    W = -(-(LATW + R) // 128) * 128
    if first:
        qn, qr, wk = queries
        H = qn.shape[1]
    else:
        H = queries[0].shape[1] // B
    HB = H * B
    vm = pl.BlockSpec(memory_space=pltpu.VMEM)
    hbm = pl.BlockSpec(memory_space=pltpu.HBM)
    bf, f32 = jnp.bfloat16, jnp.float32
    in_specs = [pl.BlockSpec(memory_space=pltpu.SMEM)] + ([hbm] * 3 if first else [vm] * 4)
    keep = lambda xs, space: [pltpu.with_memory_space_constraint(x, space) for x in xs]
    args = [pos, *keep(queries, pltpu.HBM if first else pltpu.VMEM)]
    if last:
        in_specs.append(hbm)
        args += keep([w_uv], pltpu.HBM)
    in_specs += [vm] * len(shards)
    args += keep(shards, pltpu.VMEM)
    again = state is not None
    aliases = {}
    if first and not last:
        if again:
            aliases = {len(args) + i: i for i in range(4)}
            in_specs += [vm] * 4
            args += keep(state, pltpu.VMEM)
        else:
            aliases = {}
    q_shape = (2, HB, W)
    if last:
        out_shape = jax.ShapeDtypeStruct((T, H, w_uv.shape[2]), bf)
        out_specs = hbm
        scratch = [pltpu.VMEM(q_shape, bf)] if first else []
    else:
        out_shape = [
            pltpu.VMEM(q_shape, bf),
            pltpu.VMEM((2, HB, B), f32),
            pltpu.VMEM((2, HB, B), f32),
            pltpu.VMEM((2, HB, LATW), f32),
        ]
        if not first:
            out_shape = out_shape[1:]
        elif not again:
            out_shape.append(pltpu.VMEM(shards[0].shape, bf))
        out_specs = [vm] * len(out_shape)
        scratch = []
    scratch += [
        pltpu.VMEM((2 * ns, W, B), bf),
        pltpu.VMEM((2 * ns, B, LATW), bf),
        pltpu.SMEM((16,), jnp.int32),
        pltpu.SMEM((16,), jnp.int32),
    ]
    if first:
        scratch += [
            pltpu.VMEM(qn.shape, bf),
            pltpu.VMEM(qr.shape, bf),
            pltpu.VMEM(wk.shape, bf),
            pltpu.VMEM((T * H, qn.shape[2]), f32),
            pltpu.SemaphoreType.DMA((3,)),
        ]
    if last:
        scratch += [
            pltpu.VMEM(w_uv.shape, bf),
            pltpu.VMEM((2, HB, LATW), bf),
            pltpu.VMEM((T * H, w_uv.shape[2]), f32),
            pltpu.VMEM((T, H, w_uv.shape[2]), bf),
            pltpu.SemaphoreType.DMA,
            pltpu.SemaphoreType.DMA((2,)),
        ]
    made = pl.pallas_call(
        functools.partial(phase_kernel, first, last, offsets, ns, split, when, again),
        out_shape=out_shape,
        in_specs=in_specs,
        out_specs=out_specs,
        scratch_shapes=scratch,
        input_output_aliases=aliases,
        compiler_params=pltpu.CompilerParams(vmem_limit_bytes=limit * MIB),
        cost_estimate=pl.CostEstimate(flops=int(FL * ns), bytes_accessed=4 * MIB, transcendentals=MIB),
        name="first" if first else "last" if last else "middle",
    )(*args)
    return made if first or last else [queries[0], *made]


def pack_kernel(c_h, r_h, out, sem):
    rows = c_h.shape[0]
    half = r_h.shape[0] // 2
    copies = [
        pltpu.make_async_copy(c_h, out.at[pl.ds(0, rows), :], sem.at[0]),
        pltpu.make_async_copy(r_h.at[pl.ds(0, half), :], out.at[pl.ds(rows, half), pl.ds(0, rows)], sem.at[1]),
        pltpu.make_async_copy(r_h.at[pl.ds(half, half), :], out.at[pl.ds(rows, half), pl.ds(rows, rows)], sem.at[2]),
    ]
    for copy in copies:
        copy.start()
    for copy in copies:
        copy.wait()


def pack(c_kv, k_rope_t):
    rows, width = c_kv.shape
    hbm = pl.BlockSpec(memory_space=pltpu.HBM)
    return pl.pallas_call(
        pack_kernel,
        out_shape=pltpu.VMEM((rows + k_rope_t.shape[0] // 2, width), c_kv.dtype),
        in_specs=[hbm, hbm],
        out_specs=pl.BlockSpec(memory_space=pltpu.VMEM),
        scratch_shapes=[pltpu.SemaphoreType.DMA((3,))],
        compiler_params=pltpu.CompilerParams(vmem_limit_bytes=2 * MIB),
        name="pack",
    )(*[pltpu.with_memory_space_constraint(x, pltpu.HBM) for x in (c_kv, k_rope_t)])


def hold_kernel(one, _, out):
    out[...] = one[...]


def hold(one, after):
    vm = pl.BlockSpec(memory_space=pltpu.VMEM)
    return pl.pallas_call(
        hold_kernel,
        out_shape=pltpu.VMEM(one.shape, one.dtype),
        in_specs=[vm, vm],
        out_specs=vm,
        compiler_params=pltpu.CompilerParams(vmem_limit_bytes=2 * MIB),
        name="hold",
    )(*[pltpu.with_memory_space_constraint(x, pltpu.VMEM) for x in (one, after)])


def pairs(n, heads, source):
    out = []
    for t in range(n):
        s = source(t)
        if s is None:
            continue
        s %= n
        for h in range(heads):
            hs = h if s // 4 == t // 4 or abs(s - t) > n // 2 else heads - 1 - h
            out.append((s * heads + hs, t * heads + h))
    return out


def per_device(q_nope, q_rope, c_kv, k_rope, block_pos, w_uk, w_uv):
    n, heads = lax.axis_size("ctx"), lax.axis_size("head")
    send = lambda x, source: lax.ppermute(x, ("ctx", "head"), pairs(n, heads, source))
    mine = pack(c_kv, k_rope.T)
    queries = (q_nope, jnp.transpose(q_rope, (1, 2, 0)), w_uk)
    side = lambda place: 2 * lax.rem(place, 2) - 1
    swap = lambda t: t ^ 1
    near = lambda place: (0,)
    below = send(mine, lambda t: t - 2)
    *state, mine = phase(True, False, near, block_pos, queries, None, [mine], when=lambda p: p < 2)
    above = send(mine, lambda t: t + 2)
    mate = send(mine, swap)
    state = phase(True, False, near, block_pos, queries, None, [mine], when=lambda p: p >= 2, state=state)
    cross_b = send(hold(below, state[1]), lambda t: t + 1 if t % 2 == 0 else None)
    cross_a = send(hold(above, state[1]), lambda t: t - 1 if t % 2 else None)
    return phase(False, True, lambda p: (side(p), 2, -2, -side(p)), block_pos, state, w_uv, [mate, below, above, (cross_b, cross_a)])


def solution(mesh):
    placed = (
        P("ctx", "head", None),
        P("ctx", "head", None),
        P("ctx", None),
        P("ctx", None),
        P(),
        P("head", None, None),
        P("head", None, None),
    )
    return jax.shard_map(
        per_device, mesh=mesh, in_specs=placed, out_specs=P("ctx", "head", None), check_vma=False
    )
```

```python
import functools
import math

import jax
import jax.numpy as jnp
from jax import lax
from jax.experimental import pallas as pl
from jax.experimental.pallas import tpu as pltpu
from jax.sharding import PartitionSpec as P

NEG = -1e30
LOG2E = 1.4426950408889634
CHUNK = 256
AHEAD = 3
MIB = 1024 * 1024
FL = 4e9


def place_now():
    return lax.axis_index("ctx")


def phase_kernel(first, last, offsets, where, packed, when, again, *refs):
    refs = list(refs)
    take = lambda k: [refs.pop(0) for _ in range(k)]
    (pos,) = take(1)
    if first:
        qn_h, qr_h, wk_h = take(3)
    else:
        qs, m_in, l_in, o_in = take(4)
    if last:
        (wv_h,) = take(1)
    ns = len(where)
    arrays = take(1 + max(k for parts in where for k, _ in parts))
    shards = [[(arrays[k], start) for k, start in parts] for parts in where]
    if first and again:
        take(4)
    if last:
        (out_h,) = take(1)
        if first:
            (qs,) = take(1)
    else:
        if first:
            (qs,) = take(1)
        m_out, l_out, o_out = take(3)
        if first and not again:
            (passed,) = take(1)
            passed[...] = arrays[0][...]
    kt, vs, low_l, high_l = take(4)
    copies = []
    if first:
        qn, qr, wk, qf, sem_q = take(5)
        copies = [
            pltpu.make_async_copy(qn_h, qn, sem_q.at[0]),
            pltpu.make_async_copy(wk_h, wk, sem_q.at[1]),
            pltpu.make_async_copy(qr_h, qr, sem_q.at[2]),
        ]
    if last:
        wv, os_, of, ob, sem_w, sem_o = take(6)
        copy_w = pltpu.make_async_copy(wv_h, wv, sem_w)
    def run():
        for copy in copies:
            copy.start()
        if last:
            copy_w.start()

        _, HB, W = qs.shape
        B = kt.shape[2]
        LATW = vs.shape[2]
        T = 2 * B
        H = HB // B
        R = 2 * (packed - T)
        c2 = LOG2E / math.sqrt(LATW // 4 + R)
        place = place_now()
        nctx = pos.shape[0] // 2

        def a_of(off):
            return pos[2 * lax.rem(place - off + nctx, nctx)]

        mine = a_of(0)
        nl = jnp.int32(0)
        nh = jnp.int32(0)
        for i, off in enumerate(offsets(place)):
            if first and i == 0:
                low_l[nl] = 0
                high_l[nh] = 0
                high_l[nh + 1] = 1
                nl, nh = nl + 1, nh + 2
            else:
                lt = (a_of(off) < mine).astype(jnp.int32)
                low_l[nl] = 2 * i
                nl = nl + lt
                high_l[nh] = 2 * i
                high_l[nh + 1] = 2 * i + 1
                nh = nh + 2 - lt
        low_l[nl] = 0
        high_l[nh] = 0

        zero_k = jnp.zeros((W - LATW - R, B), jnp.bfloat16)
        for i, parts in enumerate(shards):
            def rows_of(lo, hi):
                got = [ref[start + lo:start + hi, :] for ref, start in parts]
                return functools.reduce(lambda x, y: x + y, got)

            rope = rows_of(T, T + R // 2)
            rope = jnp.concatenate([rope[:, :T], rope[:, T:]], axis=0)
            for b in range(2):
                c = rows_of(b * B, (b + 1) * B)
                vs[2 * i + b] = c
                kt[2 * i + b, :LATW, :] = c.T
                kt[2 * i + b, LATW:LATW + R, :] = rope[:, b * B:(b + 1) * B]
                kt[2 * i + b, LATW + R:, :] = zero_k

        if first:
            N = wk.shape[1]
            copies[0].wait()
            qf[...] = qn[...].astype(jnp.float32).reshape(T * H, N)
            zero_q = jnp.zeros((B, W - LATW - R), jnp.bfloat16)
            copies[1].wait()
            copies[2].wait()
            for h in range(H):
                q = qf[pl.ds(h, T, stride=H), :].astype(jnp.bfloat16)
                ql = jnp.dot(q, wk[h], preferred_element_type=jnp.float32).astype(jnp.bfloat16)
                qrt = qr[h].T
                for b in range(2):
                    rr = slice(h * B, (h + 1) * B)
                    qs[b, rr, :LATW] = ql[b * B:(b + 1) * B]
                    qs[b, rr, LATW:LATW + R] = qrt[b * B:(b + 1) * B]
                    qs[b, rr, LATW + R:] = zero_q

        def process(*jobs):
            rows = []
            for half, n, lst, nb in jobs:
                k_items = []
                v_items = []
                for i in range(n):
                    b0, b1 = lst[2 * i], lst[2 * i + 1]
                    k_items.append(jnp.concatenate([kt[b0], kt[b1]], axis=1))
                    v_items.append(jnp.concatenate([vs[b0], vs[b1]], axis=0))
                for r in range(HB // CHUNK):
                    rows.append((half, slice(r * CHUNK, (r + 1) * CHUNK), n, nb, k_items, v_items))

            def scores(half, rr, n, nb, k_items, v_items):
                parts = []
                q = qs[half, rr, :]
                for i in range(n):
                    s = jnp.dot(q, k_items[i], preferred_element_type=jnp.float32)
                    s0, s1 = s[:, :B], s[:, B:]
                    if first and i == 0:
                        t_id = lax.broadcasted_iota(jnp.int32, (CHUNK, B), 0) % B
                        k_id = lax.broadcasted_iota(jnp.int32, (CHUNK, B), 1)
                        if half == 0:
                            s0 = jnp.where(k_id <= t_id, s0, NEG)
                        else:
                            s1 = jnp.where(k_id <= t_id, s1, NEG)
                    if nb is not None and i == n - 1:
                        s1 = jnp.where(nb == 2 * n, s1, NEG)
                    parts += [s0, s1]
                return parts

            def weigh(part, half, rr, n, nb, k_items, v_items):
                if n == 0:
                    return m_in[half, rr, :1], l_in[half, rr, :], o_in[half, rr, :]
                mx = part[0]
                for j in range(1, 2 * n):
                    mx = jnp.maximum(mx, part[j])
                m = jnp.max(mx, axis=1, keepdims=True)
                if first:
                    l = jnp.zeros((CHUNK, B), jnp.float32)
                else:
                    old = m_in[half, rr, :1]
                    m = jnp.maximum(m, old)
                    alpha = jnp.exp2((old - m) * c2)
                    l = l_in[half, rr, :] * alpha
                ps = []
                for j in range(2 * n):
                    p = jnp.exp2((part[j] - m) * c2)
                    l = l + p
                    ps.append(p.astype(jnp.bfloat16))
                o = jnp.dot(
                    jnp.concatenate(ps, axis=1), jnp.concatenate(v_items, axis=0), preferred_element_type=jnp.float32
                )
                if not first:
                    o = o + o_in[half, rr, :] * alpha
                return m, l, o

            def keep(half, rr, m, l, o):
                if last:
                    inv = 1.0 / jnp.sum(l, axis=1, keepdims=True)
                    os_[half, rr, :] = (o * inv).astype(jnp.bfloat16)
                else:
                    m_out[half, rr, :] = jnp.broadcast_to(m, (CHUNK, B))
                    l_out[half, rr, :] = l
                    o_out[half, rr, :] = o

            waiting = [scores(*row) for row in rows[:AHEAD]]
            for r, row in enumerate(rows):
                if r + AHEAD < len(rows):
                    waiting.append(scores(*rows[r + AHEAD]))
                keep(*row[:2], *weigh(waiting[r], *row))
                if last and (r + 1 == len(rows) or rows[r + 1][0] != row[0]):
                    output(row[0])

        def output(half):
            if half == 0:
                copy_w.wait()
            for h in range(H):
                o = os_[half, h * B:(h + 1) * B, :]
                of[pl.ds(half * HB + h, B, stride=H), :] = jnp.dot(o, wv[h], preferred_element_type=jnp.float32)
            rows = slice(half * HB, (half + 1) * HB)
            ob[half * B:(half + 1) * B] = of[rows, :].reshape(B, H, of.shape[1]).astype(jnp.bfloat16)
            out_copy(half).start()

        def out_copy(half):
            return pltpu.make_async_copy(ob.at[pl.ds(half * B, B)], out_h.at[pl.ds(half * B, B)], sem_o.at[half])

        if first:
            counts = [((2 + j) // 2, (2 * ns - j + 1) // 2) for j in range(ns)]
        else:
            counts = [((j + 1) // 2, (2 * ns - j + 1) // 2) for j in range(ns + 1)]
        if len(counts) == 1:
            process((0, counts[0][0], low_l, nl), (1, counts[0][1], high_l, nh))
        elif ns == 4:
            usual = nl == 2
            pl.when(usual)(lambda: process((0, *counts[2][:1], low_l, None), (1, counts[2][1], high_l, None)))
            for half, lst, nb in ((0, low_l, nl), (1, high_l, nh)):
                items = (nb + 1) // 2
                for n in sorted({c[half] for j, c in enumerate(counts) if j != 2}):
                    pl.when((items == n) & (nl != 2))(functools.partial(process, (half, n, lst, nb)))
        else:
            for half, lst, nb in ((0, low_l, nl), (1, high_l, nh)):
                items = (nb + 1) // 2
                for n in sorted({c[half] for c in counts}):
                    pl.when(items == n)(functools.partial(process, (half, n, lst, nb)))
        if last:
            for half in range(2):
                out_copy(half).wait()

    if when is None:
        run()
    else:
        pl.when(when(place_now()))(run)


def phase(first, last, offsets, pos, queries, w_uv, shards, where, when=None, state=None, limit=14):
    ns = len(where)
    T = 256
    B = T // 2
    LATW = shards[0].shape[1]
    packed = shards[0].shape[0]
    R = 2 * (packed - T)
    W = -(-(LATW + R) // 128) * 128
    if first:
        qn, qr, wk = queries
        H = qn.shape[1]
    else:
        H = queries[0].shape[1] // B
    HB = H * B
    vm = pl.BlockSpec(memory_space=pltpu.VMEM)
    hbm = pl.BlockSpec(memory_space=pltpu.HBM)
    bf, f32 = jnp.bfloat16, jnp.float32
    in_specs = [pl.BlockSpec(memory_space=pltpu.SMEM)] + ([hbm] * 3 if first else [vm] * 4)
    keep = lambda xs, space: [pltpu.with_memory_space_constraint(x, space) for x in xs]
    args = [pos, *keep(queries, pltpu.HBM if first else pltpu.VMEM)]
    if last:
        in_specs.append(hbm)
        args += keep([w_uv], pltpu.HBM)
    in_specs += [vm] * len(shards)
    args += keep(shards, pltpu.VMEM)
    again = state is not None
    aliases = {}
    if first and not last:
        if again:
            aliases = {len(args) + i: i for i in range(4)}
            in_specs += [vm] * 4
            args += keep(state, pltpu.VMEM)
        else:
            aliases = {}
    q_shape = (2, HB, W)
    if last:
        out_shape = jax.ShapeDtypeStruct((T, H, w_uv.shape[2]), bf)
        out_specs = hbm
        scratch = [pltpu.VMEM(q_shape, bf)] if first else []
    else:
        out_shape = [
            pltpu.VMEM(q_shape, bf),
            pltpu.VMEM((2, HB, B), f32),
            pltpu.VMEM((2, HB, B), f32),
            pltpu.VMEM((2, HB, LATW), f32),
        ]
        if not first:
            out_shape = out_shape[1:]
        elif not again:
            out_shape.append(pltpu.VMEM(shards[0].shape, bf))
        out_specs = [vm] * len(out_shape)
        scratch = []
    scratch += [
        pltpu.VMEM((2 * ns, W, B), bf),
        pltpu.VMEM((2 * ns, B, LATW), bf),
        pltpu.SMEM((16,), jnp.int32),
        pltpu.SMEM((16,), jnp.int32),
    ]
    if first:
        scratch += [
            pltpu.VMEM(qn.shape, bf),
            pltpu.VMEM(qr.shape, bf),
            pltpu.VMEM(wk.shape, bf),
            pltpu.VMEM((T * H, qn.shape[2]), f32),
            pltpu.SemaphoreType.DMA((3,)),
        ]
    if last:
        scratch += [
            pltpu.VMEM(w_uv.shape, bf),
            pltpu.VMEM((2, HB, LATW), bf),
            pltpu.VMEM((T * H, w_uv.shape[2]), f32),
            pltpu.VMEM((T, H, w_uv.shape[2]), bf),
            pltpu.SemaphoreType.DMA,
            pltpu.SemaphoreType.DMA((2,)),
        ]
    made = pl.pallas_call(
        functools.partial(phase_kernel, first, last, offsets, where, packed, when, again),
        out_shape=out_shape,
        in_specs=in_specs,
        out_specs=out_specs,
        scratch_shapes=scratch,
        input_output_aliases=aliases,
        compiler_params=pltpu.CompilerParams(vmem_limit_bytes=limit * MIB),
        cost_estimate=pl.CostEstimate(flops=int(FL * ns), bytes_accessed=4 * MIB, transcendentals=MIB),
        name="first" if first else "last" if last else "middle",
    )(*args)
    return made if first or last else [queries[0], *made]


def pack_kernel(c_h, r_h, out, sem):
    rows = c_h.shape[0]
    half = r_h.shape[0] // 2
    copies = [
        pltpu.make_async_copy(c_h, out.at[pl.ds(0, rows), :], sem.at[0]),
        pltpu.make_async_copy(r_h.at[pl.ds(0, half), :], out.at[pl.ds(rows, half), pl.ds(0, rows)], sem.at[1]),
        pltpu.make_async_copy(r_h.at[pl.ds(half, half), :], out.at[pl.ds(rows, half), pl.ds(rows, rows)], sem.at[2]),
    ]
    for copy in copies:
        copy.start()
    for copy in copies:
        copy.wait()


def pack(c_kv, k_rope_t):
    rows, width = c_kv.shape
    hbm = pl.BlockSpec(memory_space=pltpu.HBM)
    return pl.pallas_call(
        pack_kernel,
        out_shape=pltpu.VMEM((rows + k_rope_t.shape[0] // 2, width), c_kv.dtype),
        in_specs=[hbm, hbm],
        out_specs=pl.BlockSpec(memory_space=pltpu.VMEM),
        scratch_shapes=[pltpu.SemaphoreType.DMA((3,))],
        compiler_params=pltpu.CompilerParams(vmem_limit_bytes=2 * MIB),
        name="pack",
    )(*[pltpu.with_memory_space_constraint(x, pltpu.HBM) for x in (c_kv, k_rope_t)])


def join_parity_kernel(own, even, odd, _, out):
    rows = own.shape[0]
    out[:rows, :] = own[...]
    parity = lax.rem(place_now(), 2)
    for k, array in enumerate((even, odd)):

        @pl.when(parity == k)
        def _():
            out[rows:, :] = array[...]


def join_parity(after, own, even, odd):
    vm = pl.BlockSpec(memory_space=pltpu.VMEM)
    rows, width = own.shape
    return pl.pallas_call(
        join_parity_kernel,
        out_shape=pltpu.VMEM((2 * rows, width), own.dtype),
        in_specs=[vm] * 4,
        out_specs=vm,
        compiler_params=pltpu.CompilerParams(vmem_limit_bytes=2 * MIB),
        name="join_parity",
    )(*[pltpu.with_memory_space_constraint(x, pltpu.VMEM) for x in (own, even, odd, after)])


def join_kernel(*refs):
    *arrays, _, out = refs
    rows = arrays[0].shape[0]
    for i, array in enumerate(arrays):
        out[i * rows:(i + 1) * rows, :] = array[...]


def join(after, *arrays):
    vm = pl.BlockSpec(memory_space=pltpu.VMEM)
    rows, width = arrays[0].shape
    return pl.pallas_call(
        join_kernel,
        out_shape=pltpu.VMEM((len(arrays) * rows, width), arrays[0].dtype),
        in_specs=[vm] * (1 + len(arrays)),
        out_specs=vm,
        compiler_params=pltpu.CompilerParams(vmem_limit_bytes=2 * MIB),
        name="join",
    )(*[pltpu.with_memory_space_constraint(x, pltpu.VMEM) for x in (*arrays, after)])


def pairs(n, heads, source):
    out = []
    for t in range(n):
        s = source(t)
        if s is None:
            continue
        s %= n
        for h in range(heads):
            hs = h if s // 4 == t // 4 or s // 16 != t // 16 else heads - 1 - h
            out.append((s * heads + hs, t * heads + h))
    return out


def per_device(q_nope, q_rope, c_kv, k_rope, block_pos, w_uk, w_uv):
    n, heads = lax.axis_size("ctx"), lax.axis_size("head")
    send = lambda x, source: lax.ppermute(x, ("ctx", "head"), pairs(n, heads, source))
    mine = pack(c_kv, k_rope.T)
    rows = mine.shape[0]
    queries = (q_nope, jnp.transpose(q_rope, (1, 2, 0)), w_uk)
    side = lambda place: 2 * lax.rem(place, 2) - 1
    near = lambda place: (0,)
    own = [[(0, 0)]]
    below = send(mine, lambda t: t - 2)
    above = send(mine, lambda t: t + 2 if t < n - 4 else None)
    *state, mine = phase(True, False, near, block_pos, queries, w_uv, [mine], own, when=lambda p: p < 2)
    turn = send(mine, lambda t: t + 2 if t >= n - 4 else None)
    state = phase(
        True, False, near, block_pos, queries, w_uv, [mine], own, when=lambda p: p >= 2, state=state
    )
    mate = send(join_parity(state[1], mine, above, below), lambda t: t ^ 1)
    to_end = send(join(state[1], turn), lambda t: t - 1 if t >= n - 4 and t % 2 else None)
    return phase(
        False,
        True,
        lambda p: (side(p), 2, -2, -side(p)),
        block_pos,
        state,
        w_uv,
        [below, above, turn, mate, to_end],
        [[(3, 0)], [(0, 0)], [(1, 0), (2, 0)], [(3, rows), (4, 0)]],
    )


def solution(mesh):
    placed = (
        P("ctx", "head", None),
        P("ctx", "head", None),
        P("ctx", None),
        P("ctx", None),
        P(),
        P("head", None, None),
        P("head", None, None),
    )
    return jax.shard_map(
        per_device, mesh=mesh, in_specs=placed, out_specs=P("ctx", "head", None), check_vma=False
    )
```

```python
import functools
import math

import jax
import jax.numpy as jnp
from jax import lax
from jax.experimental import pallas as pl
from jax.experimental.pallas import tpu as pltpu
from jax.sharding import PartitionSpec as P

NEG = -1e30
LOG2E = 1.4426950408889634
CHUNK = 256
AHEAD = 4
MIB = 1024 * 1024
FL = 4e9


def place_now():
    return lax.axis_index("ctx")


def phase_kernel(first, last, offsets, where, packed, when, again, *refs):
    refs = list(refs)
    take = lambda k: [refs.pop(0) for _ in range(k)]
    if not first:
        (pos_h,) = take(1)
    if first:
        qn_h, qr_h, wk_h = take(3)
    else:
        qs, m_in, l_in, o_in = take(4)
    if last:
        (wv_h,) = take(1)
    ns = len(where)
    arrays = take(1 + max(k for parts in where for k, _ in parts))
    shards = [[(arrays[k], start) for k, start in parts] for parts in where]
    if first and again:
        take(4)
    if last:
        (out_h,) = take(1)
        if first:
            (qs,) = take(1)
    else:
        if first:
            (qs,) = take(1)
        m_out, l_out, o_out = take(3)
        if first and not again:
            (passed,) = take(1)
            passed[...] = arrays[0][...]
    kt, vs, low_l, high_l = take(4)
    if not first:
        pos, sem_p = take(2)
    copies = []
    if first:
        qn, qr, wk, qf, sem_q = take(5)
        copies = [
            pltpu.make_async_copy(qn_h, qn, sem_q.at[0]),
            pltpu.make_async_copy(wk_h, wk, sem_q.at[1]),
            pltpu.make_async_copy(qr_h, qr, sem_q.at[2]),
        ]
    if last:
        wv, os_, of, ob, sem_w, sem_o = take(6)
        copy_w = pltpu.make_async_copy(wv_h, wv, sem_w)
    def run():
        if not first:
            copy_p = pltpu.make_async_copy(pos_h, pos, sem_p)
            copy_p.start()
        for copy in copies:
            copy.start()
        if last:
            copy_w.start()

        _, HB, W = qs.shape
        B = kt.shape[2]
        LATW = vs.shape[2]
        T = 2 * B
        H = HB // B
        R = 2 * (packed - T)
        c2 = LOG2E / math.sqrt(LATW // 4 + R)
        place = place_now()

        zero_k = jnp.zeros((W - LATW - R, B), jnp.bfloat16)
        for i, parts in enumerate(shards):
            def rows_of(lo, hi):
                got = [ref[start + lo:start + hi, :] for ref, start in parts]
                return functools.reduce(lambda x, y: x + y, got)

            rope = rows_of(T, T + R // 2)
            rope = jnp.concatenate([rope[:, :T], rope[:, T:]], axis=0)
            for b in range(2):
                c = rows_of(b * B, (b + 1) * B)
                vs[2 * i + b] = c
                kt[2 * i + b, :LATW, :] = c.T
                kt[2 * i + b, LATW:LATW + R, :] = rope[:, b * B:(b + 1) * B]
                kt[2 * i + b, LATW + R:, :] = zero_k

        def a_of(off):
            nctx = pos.shape[0] // 2
            return pos[2 * lax.rem(place - off + nctx, nctx)]

        if not first:
            copy_p.wait()
            mine = a_of(0)
        nl = jnp.int32(0)
        nh = jnp.int32(0)
        for i, off in enumerate(offsets(place)):
            if first and i == 0:
                low_l[nl] = 0
                high_l[nh] = 0
                high_l[nh + 1] = 1
                nl, nh = nl + 1, nh + 2
            else:
                lt = (a_of(off) < mine).astype(jnp.int32)
                low_l[nl] = 2 * i
                nl = nl + lt
                high_l[nh] = 2 * i
                high_l[nh + 1] = 2 * i + 1
                nh = nh + 2 - lt
        low_l[nl] = 0
        high_l[nh] = 0

        if first:
            N = wk.shape[1]
            copies[0].wait()
            qf[...] = qn[...].astype(jnp.float32).reshape(T * H, N)
            zero_q = jnp.zeros((B, W - LATW - R), jnp.bfloat16)
            copies[1].wait()
            copies[2].wait()
            for h in range(H):
                q = qf[pl.ds(h, T, stride=H), :].astype(jnp.bfloat16)
                ql = jnp.dot(q, wk[h], preferred_element_type=jnp.float32).astype(jnp.bfloat16)
                qrt = qr[h].T
                for b in range(2):
                    rr = slice(h * B, (h + 1) * B)
                    qs[b, rr, :LATW] = ql[b * B:(b + 1) * B]
                    qs[b, rr, LATW:LATW + R] = qrt[b * B:(b + 1) * B]
                    qs[b, rr, LATW + R:] = zero_q

        def process(*jobs):
            rows = []
            for half, n, lst, nb in jobs:
                k_items = []
                v_items = []
                for i in range(n):
                    b0, b1 = lst[2 * i], lst[2 * i + 1]
                    k_items.append(jnp.concatenate([kt[b0], kt[b1]], axis=1))
                    v_items.append(jnp.concatenate([vs[b0], vs[b1]], axis=0))
                for r in range(HB // CHUNK):
                    rows.append((half, slice(r * CHUNK, (r + 1) * CHUNK), n, nb, k_items, v_items))

            def scores(half, rr, n, nb, k_items, v_items):
                parts = []
                q = qs[half, rr, :]
                for i in range(n):
                    s = jnp.dot(q, k_items[i], preferred_element_type=jnp.float32)
                    s0, s1 = s[:, :B], s[:, B:]
                    if first and i == 0:
                        t_id = lax.broadcasted_iota(jnp.int32, (CHUNK, B), 0) % B
                        k_id = lax.broadcasted_iota(jnp.int32, (CHUNK, B), 1)
                        if half == 0:
                            s0 = jnp.where(k_id <= t_id, s0, NEG)
                        else:
                            s1 = jnp.where(k_id <= t_id, s1, NEG)
                    if nb is not None and i == n - 1:
                        s1 = jnp.where(nb == 2 * n, s1, NEG)
                    parts += [s0, s1]
                return parts

            def weigh(part, half, rr, n, nb, k_items, v_items):
                if n == 0:
                    return m_in[half, rr, :1], l_in[half, rr, :], o_in[half, rr, :]
                mx = part[0]
                for j in range(1, 2 * n):
                    mx = jnp.maximum(mx, part[j])
                m = jnp.max(mx, axis=1, keepdims=True)
                if first:
                    l = jnp.zeros((CHUNK, B), jnp.float32)
                else:
                    old = m_in[half, rr, :1]
                    m = jnp.maximum(m, old)
                    alpha = jnp.exp2((old - m) * c2)
                    l = l_in[half, rr, :] * alpha
                ps = []
                for j in range(2 * n):
                    p = jnp.exp2((part[j] - m) * c2)
                    l = l + p
                    ps.append(p.astype(jnp.bfloat16))
                o = jnp.dot(
                    jnp.concatenate(ps, axis=1), jnp.concatenate(v_items, axis=0), preferred_element_type=jnp.float32
                )
                if not first:
                    o = o + o_in[half, rr, :] * alpha
                return m, l, o

            def keep(half, rr, m, l, o):
                if last:
                    inv = 1.0 / jnp.sum(l, axis=1, keepdims=True)
                    os_[half, rr, :] = (o * inv).astype(jnp.bfloat16)
                else:
                    m_out[half, rr, :] = jnp.broadcast_to(m, (CHUNK, B))
                    l_out[half, rr, :] = l
                    o_out[half, rr, :] = o

            waiting = [scores(*row) for row in rows[:AHEAD]]
            for r, row in enumerate(rows):
                if r + AHEAD < len(rows):
                    waiting.append(scores(*rows[r + AHEAD]))
                keep(*row[:2], *weigh(waiting[r], *row))
                if last and (r + 1 == len(rows) or rows[r + 1][0] != row[0]):
                    output(row[0])

        def output(half):
            if half == 0:
                copy_w.wait()
            for h in range(H):
                o = os_[half, h * B:(h + 1) * B, :]
                of[pl.ds(half * HB + h, B, stride=H), :] = jnp.dot(o, wv[h], preferred_element_type=jnp.float32)
            rows = slice(half * HB, (half + 1) * HB)
            ob[half * B:(half + 1) * B] = of[rows, :].reshape(B, H, of.shape[1]).astype(jnp.bfloat16)
            out_copy(half).start()

        def out_copy(half):
            return pltpu.make_async_copy(ob.at[pl.ds(half * B, B)], out_h.at[pl.ds(half * B, B)], sem_o.at[half])

        if first:
            counts = [((2 + j) // 2, (2 * ns - j + 1) // 2) for j in range(ns)]
        else:
            counts = [((j + 1) // 2, (2 * ns - j + 1) // 2) for j in range(ns + 1)]
        if len(counts) == 1:
            process((0, counts[0][0], low_l, nl), (1, counts[0][1], high_l, nh))
        elif ns == 4:
            usual = nl == 2
            pl.when(usual)(lambda: process((0, *counts[2][:1], low_l, None), (1, counts[2][1], high_l, None)))
            for half, lst, nb in ((0, low_l, nl), (1, high_l, nh)):
                items = (nb + 1) // 2
                for n in sorted({c[half] for j, c in enumerate(counts) if j != 2}):
                    pl.when((items == n) & (nl != 2))(functools.partial(process, (half, n, lst, nb)))
        else:
            for half, lst, nb in ((0, low_l, nl), (1, high_l, nh)):
                items = (nb + 1) // 2
                for n in sorted({c[half] for c in counts}):
                    pl.when(items == n)(functools.partial(process, (half, n, lst, nb)))
        if last:
            for half in range(2):
                out_copy(half).wait()

    if when is None:
        run()
    else:
        pl.when(when(place_now()))(run)


def phase(first, last, offsets, pos, queries, w_uv, shards, where, when=None, state=None, limit=14):
    ns = len(where)
    T = 256
    B = T // 2
    LATW = shards[0].shape[1]
    packed = shards[0].shape[0]
    R = 2 * (packed - T)
    W = -(-(LATW + R) // 128) * 128
    if first:
        qn, qr, wk = queries
        H = qn.shape[1]
    else:
        H = queries[0].shape[1] // B
    HB = H * B
    vm = pl.BlockSpec(memory_space=pltpu.VMEM)
    hbm = pl.BlockSpec(memory_space=pltpu.HBM)
    bf, f32 = jnp.bfloat16, jnp.float32
    in_specs = [hbm] * 3 if first else [hbm] + [vm] * 4
    keep = lambda xs, space: [pltpu.with_memory_space_constraint(x, space) for x in xs]
    args = keep(queries, pltpu.HBM) if first else [*keep([pos], pltpu.HBM), *keep(queries, pltpu.VMEM)]
    if last:
        in_specs.append(hbm)
        args += keep([w_uv], pltpu.HBM)
    in_specs += [vm] * len(shards)
    args += keep(shards, pltpu.VMEM)
    again = state is not None
    aliases = {}
    if first and not last:
        if again:
            aliases = {len(args) + i: i for i in range(4)}
            in_specs += [vm] * 4
            args += keep(state, pltpu.VMEM)
        else:
            aliases = {}
    q_shape = (2, HB, W)
    if last:
        out_shape = jax.ShapeDtypeStruct((T, H, w_uv.shape[2]), bf)
        out_specs = hbm
        scratch = [pltpu.VMEM(q_shape, bf)] if first else []
    else:
        out_shape = [
            pltpu.VMEM(q_shape, bf),
            pltpu.VMEM((2, HB, B), f32),
            pltpu.VMEM((2, HB, B), f32),
            pltpu.VMEM((2, HB, LATW), f32),
        ]
        if not first:
            out_shape = out_shape[1:]
        elif not again:
            out_shape.append(pltpu.VMEM(shards[0].shape, bf))
        out_specs = [vm] * len(out_shape)
        scratch = []
    scratch += [
        pltpu.VMEM((2 * ns, W, B), bf),
        pltpu.VMEM((2 * ns, B, LATW), bf),
        pltpu.SMEM((16,), jnp.int32),
        pltpu.SMEM((16,), jnp.int32),
    ]
    if not first:
        scratch += [pltpu.SMEM(pos.shape, jnp.int32), pltpu.SemaphoreType.DMA]
    if first:
        scratch += [
            pltpu.VMEM(qn.shape, bf),
            pltpu.VMEM(qr.shape, bf),
            pltpu.VMEM(wk.shape, bf),
            pltpu.VMEM((T * H, qn.shape[2]), f32),
            pltpu.SemaphoreType.DMA((3,)),
        ]
    if last:
        scratch += [
            pltpu.VMEM(w_uv.shape, bf),
            pltpu.VMEM((2, HB, LATW), bf),
            pltpu.VMEM((T * H, w_uv.shape[2]), f32),
            pltpu.VMEM((T, H, w_uv.shape[2]), bf),
            pltpu.SemaphoreType.DMA,
            pltpu.SemaphoreType.DMA((2,)),
        ]
    made = pl.pallas_call(
        functools.partial(phase_kernel, first, last, offsets, where, packed, when, again),
        out_shape=out_shape,
        in_specs=in_specs,
        out_specs=out_specs,
        scratch_shapes=scratch,
        input_output_aliases=aliases,
        compiler_params=pltpu.CompilerParams(vmem_limit_bytes=limit * MIB),
        cost_estimate=pl.CostEstimate(flops=int(FL * ns), bytes_accessed=4 * MIB, transcendentals=MIB),
        name="first" if first else "last" if last else "middle",
    )(*args)
    return made if first or last else [queries[0], *made]


def pack_kernel(c_h, r_h, out, sem):
    rows = c_h.shape[0]
    half = r_h.shape[0] // 2
    copies = [
        pltpu.make_async_copy(c_h, out.at[pl.ds(0, rows), :], sem.at[0]),
        pltpu.make_async_copy(r_h.at[pl.ds(0, half), :], out.at[pl.ds(rows, half), pl.ds(0, rows)], sem.at[1]),
        pltpu.make_async_copy(r_h.at[pl.ds(half, half), :], out.at[pl.ds(rows, half), pl.ds(rows, rows)], sem.at[2]),
    ]
    for copy in copies:
        copy.start()
    for copy in copies:
        copy.wait()


def pack(c_kv, k_rope_t):
    rows, width = c_kv.shape
    hbm = pl.BlockSpec(memory_space=pltpu.HBM)
    return pl.pallas_call(
        pack_kernel,
        out_shape=pltpu.VMEM((rows + k_rope_t.shape[0] // 2, width), c_kv.dtype),
        in_specs=[hbm, hbm],
        out_specs=pl.BlockSpec(memory_space=pltpu.VMEM),
        scratch_shapes=[pltpu.SemaphoreType.DMA((3,))],
        compiler_params=pltpu.CompilerParams(vmem_limit_bytes=2 * MIB),
        name="pack",
    )(*[pltpu.with_memory_space_constraint(x, pltpu.HBM) for x in (c_kv, k_rope_t)])


def join_parity_kernel(own, even, odd, _, out):
    rows = own.shape[0]
    out[:rows, :] = own[...]
    parity = lax.rem(place_now(), 2)
    for k, array in enumerate((even, odd)):

        @pl.when(parity == k)
        def _():
            out[rows:, :] = array[...]


def join_parity(after, own, even, odd):
    vm = pl.BlockSpec(memory_space=pltpu.VMEM)
    rows, width = own.shape
    return pl.pallas_call(
        join_parity_kernel,
        out_shape=pltpu.VMEM((2 * rows, width), own.dtype),
        in_specs=[vm] * 4,
        out_specs=vm,
        compiler_params=pltpu.CompilerParams(vmem_limit_bytes=2 * MIB),
        name="join_parity",
    )(*[pltpu.with_memory_space_constraint(x, pltpu.VMEM) for x in (own, even, odd, after)])


def join_kernel(*refs):
    *arrays, _, out = refs
    rows = arrays[0].shape[0]
    for i, array in enumerate(arrays):
        out[i * rows:(i + 1) * rows, :] = array[...]


def join(after, *arrays):
    vm = pl.BlockSpec(memory_space=pltpu.VMEM)
    rows, width = arrays[0].shape
    return pl.pallas_call(
        join_kernel,
        out_shape=pltpu.VMEM((len(arrays) * rows, width), arrays[0].dtype),
        in_specs=[vm] * (1 + len(arrays)),
        out_specs=vm,
        compiler_params=pltpu.CompilerParams(vmem_limit_bytes=2 * MIB),
        name="join",
    )(*[pltpu.with_memory_space_constraint(x, pltpu.VMEM) for x in (*arrays, after)])


def pairs(n, heads, source):
    out = []
    for t in range(n):
        s = source(t)
        if s is None:
            continue
        s %= n
        for h in range(heads):
            hs = h if s // 4 == t // 4 or s // 16 != t // 16 else heads - 1 - h
            out.append((s * heads + hs, t * heads + h))
    return out


def per_device(q_nope, q_rope, c_kv, k_rope, block_pos, w_uk, w_uv):
    n, heads = lax.axis_size("ctx"), lax.axis_size("head")
    send = lambda x, source: lax.ppermute(x, ("ctx", "head"), pairs(n, heads, source))
    mine = pack(c_kv, k_rope.T)
    rows = mine.shape[0]
    queries = (q_nope, jnp.transpose(q_rope, (1, 2, 0)), w_uk)
    side = lambda place: 2 * lax.rem(place, 2) - 1
    near = lambda place: (0,)
    own = [[(0, 0)]]
    below = send(mine, lambda t: t - 2)
    above = send(mine, lambda t: t + 2 if t < n - 4 else None)
    *state, mine = phase(True, False, near, block_pos, queries, w_uv, [mine], own, when=lambda p: p < 2)
    turn = send(mine, lambda t: t + 2 if t >= n - 4 else None)
    state = phase(
        True, False, near, block_pos, queries, w_uv, [mine], own, when=lambda p: p >= 2, state=state
    )
    mate = send(join_parity(state[1], mine, above, below), lambda t: t ^ 1)
    to_end = send(join(state[1], turn), lambda t: t - 1 if t >= n - 4 and t % 2 else None)
    return phase(
        False,
        True,
        lambda p: (side(p), 2, -2, -side(p)),
        block_pos,
        state,
        w_uv,
        [below, above, turn, mate, to_end],
        [[(3, 0)], [(0, 0)], [(1, 0), (2, 0)], [(3, rows), (4, 0)]],
    )


def solution(mesh):
    placed = (
        P("ctx", "head", None),
        P("ctx", "head", None),
        P("ctx", None),
        P("ctx", None),
        P(),
        P("head", None, None),
        P("head", None, None),
    )
    return jax.shard_map(
        per_device, mesh=mesh, in_specs=placed, out_specs=P("ctx", "head", None), check_vma=False
    )
```

```python
import functools
import math

import jax
import jax.numpy as jnp
from jax import lax
from jax.experimental import pallas as pl
from jax.experimental.pallas import tpu as pltpu
from jax.sharding import PartitionSpec as P

NEG = -1e30
LOG2E = 1.4426950408889634
CHUNK = 256
AHEAD = 4
PIECES = 4
MIB = 1024 * 1024
FL = 4e9


def place_now():
    return lax.axis_index("ctx")


def phase_kernel(first, last, offsets, where, packed, when, again, *refs):
    refs = list(refs)
    take = lambda k: [refs.pop(0) for _ in range(k)]
    if not first:
        (pos_h,) = take(1)
    if first:
        qn_h, qr_h, wk_h = take(3)
    else:
        qs, m_in, l_in, o_in = take(4)
    if last:
        (wv_h,) = take(1)
    ns = len(where)
    arrays = take(1 + max(k for parts in where for k, _ in parts))
    shards = [[(arrays[k], start) for k, start in parts] for parts in where]
    if first and again:
        take(4)
    if last:
        (out_h,) = take(1)
        if first:
            (qs,) = take(1)
    else:
        if first:
            (qs,) = take(1)
        m_out, l_out, o_out = take(3)
        if first and not again:
            (passed,) = take(1)
            passed[...] = arrays[0][...]
    kt, vs, low_l, high_l = take(4)
    if not first:
        pos, sem_p = take(2)
    copies = []
    if first:
        qn, qr, wk, qf, sem_q = take(5)
        copies = [
            pltpu.make_async_copy(qn_h, qn, sem_q.at[0]),
            pltpu.make_async_copy(wk_h, wk, sem_q.at[1]),
            pltpu.make_async_copy(qr_h, qr, sem_q.at[2]),
        ]
    if last:
        wv, os_, of, ob, sem_w, sem_o = take(6)
        copy_w = pltpu.make_async_copy(wv_h, wv, sem_w)
    def run():
        if not first:
            copy_p = pltpu.make_async_copy(pos_h, pos, sem_p)
            copy_p.start()
        for copy in copies:
            copy.start()
        if last:
            copy_w.start()

        _, HB, W = qs.shape
        B = kt.shape[2]
        LATW = vs.shape[2]
        T = 2 * B
        H = HB // B
        R = 2 * (packed - T)
        c2 = LOG2E / math.sqrt(LATW // 4 + R)
        place = place_now()

        zero_k = jnp.zeros((W - LATW - R, B), jnp.bfloat16)
        for i, parts in enumerate(shards):
            def rows_of(lo, hi):
                got = [ref[start + lo:start + hi, :] for ref, start in parts]
                return functools.reduce(lambda x, y: x + y, got)

            rope = rows_of(T, T + R // 2)
            rope = jnp.concatenate([rope[:, :T], rope[:, T:]], axis=0)
            for b in range(2):
                c = rows_of(b * B, (b + 1) * B)
                vs[2 * i + b] = c
                kt[2 * i + b, :LATW, :] = c.T
                kt[2 * i + b, LATW:LATW + R, :] = rope[:, b * B:(b + 1) * B]
                kt[2 * i + b, LATW + R:, :] = zero_k

        def a_of(off):
            nctx = pos.shape[0] // 2
            return pos[2 * lax.rem(place - off + nctx, nctx)]

        if not first:
            copy_p.wait()
            mine = a_of(0)
        nl = jnp.int32(0)
        nh = jnp.int32(0)
        for i, off in enumerate(offsets(place)):
            if first and i == 0:
                low_l[nl] = 0
                high_l[nh] = 0
                high_l[nh + 1] = 1
                nl, nh = nl + 1, nh + 2
            else:
                lt = (a_of(off) < mine).astype(jnp.int32)
                low_l[nl] = 2 * i
                nl = nl + lt
                high_l[nh] = 2 * i
                high_l[nh + 1] = 2 * i + 1
                nh = nh + 2 - lt
        low_l[nl] = 0
        high_l[nh] = 0

        if first:
            N = wk.shape[1]
            copies[0].wait()
            qf[...] = qn[...].astype(jnp.float32).reshape(T * H, N)
            zero_q = jnp.zeros((B, W - LATW - R), jnp.bfloat16)
            copies[1].wait()
            copies[2].wait()
            for h in range(H):
                q = qf[pl.ds(h, T, stride=H), :].astype(jnp.bfloat16)
                ql = jnp.dot(q, wk[h], preferred_element_type=jnp.float32).astype(jnp.bfloat16)
                qrt = qr[h].T
                for b in range(2):
                    rr = slice(h * B, (h + 1) * B)
                    qs[b, rr, :LATW] = ql[b * B:(b + 1) * B]
                    qs[b, rr, LATW:LATW + R] = qrt[b * B:(b + 1) * B]
                    qs[b, rr, LATW + R:] = zero_q

        def process(*jobs):
            rows = []
            for half, n, lst, nb in jobs:
                k_items = []
                v_items = []
                for i in range(n):
                    b0, b1 = lst[2 * i], lst[2 * i + 1]
                    k_items.append(jnp.concatenate([kt[b0], kt[b1]], axis=1))
                    v_items.append(jnp.concatenate([vs[b0], vs[b1]], axis=0))
                for r in range(HB // CHUNK):
                    rows.append((half, slice(r * CHUNK, (r + 1) * CHUNK), n, nb, k_items, v_items))

            def scores(half, rr, n, nb, k_items, v_items):
                parts = []
                q = qs[half, rr, :]
                for i in range(n):
                    s = jnp.dot(q, k_items[i], preferred_element_type=jnp.float32)
                    s0, s1 = s[:, :B], s[:, B:]
                    if first and i == 0:
                        t_id = lax.broadcasted_iota(jnp.int32, (CHUNK, B), 0) % B
                        k_id = lax.broadcasted_iota(jnp.int32, (CHUNK, B), 1)
                        if half == 0:
                            s0 = jnp.where(k_id <= t_id, s0, NEG)
                        else:
                            s1 = jnp.where(k_id <= t_id, s1, NEG)
                    if nb is not None and i == n - 1:
                        s1 = jnp.where(nb == 2 * n, s1, NEG)
                    parts += [s0, s1]
                return parts

            def weigh(part, half, rr, n, nb, k_items, v_items):
                if n == 0:
                    return m_in[half, rr, :1], l_in[half, rr, :], o_in[half, rr, :]
                mx = part[0]
                for j in range(1, 2 * n):
                    mx = jnp.maximum(mx, part[j])
                m = jnp.max(mx, axis=1, keepdims=True)
                if first:
                    l = jnp.zeros((CHUNK, B), jnp.float32)
                else:
                    old = m_in[half, rr, :1]
                    m = jnp.maximum(m, old)
                    alpha = jnp.exp2((old - m) * c2)
                    l = l_in[half, rr, :] * alpha
                ps = []
                for j in range(2 * n):
                    p = jnp.exp2((part[j] - m) * c2)
                    l = l + p
                    ps.append(p.astype(jnp.bfloat16))
                o = jnp.dot(
                    jnp.concatenate(ps, axis=1), jnp.concatenate(v_items, axis=0), preferred_element_type=jnp.float32
                )
                if not first:
                    o = o + o_in[half, rr, :] * alpha
                return m, l, o

            def keep(half, rr, m, l, o):
                if last:
                    inv = 1.0 / jnp.sum(l, axis=1, keepdims=True)
                    os_[half, rr, :] = (o * inv).astype(jnp.bfloat16)
                else:
                    m_out[half, rr, :] = jnp.broadcast_to(m, (CHUNK, B))
                    l_out[half, rr, :] = l
                    o_out[half, rr, :] = o

            waiting = [scores(*row) for row in rows[:AHEAD]]
            for r, row in enumerate(rows):
                if r + AHEAD < len(rows):
                    waiting.append(scores(*rows[r + AHEAD]))
                keep(*row[:2], *weigh(waiting[r], *row))
                if last and (r + 1 == len(rows) or rows[r + 1][0] != row[0]):
                    output(row[0])

        def output(half):
            if half == 0:
                copy_w.wait()
            for h in range(H):
                o = os_[half, h * B:(h + 1) * B, :]
                of[pl.ds(half * HB + h, B, stride=H), :] = jnp.dot(o, wv[h], preferred_element_type=jnp.float32)
            for k in range(PIECES):
                rows = slice(half * HB + k * HB // PIECES, half * HB + (k + 1) * HB // PIECES)
                toks = slice(half * B + k * B // PIECES, half * B + (k + 1) * B // PIECES)
                ob[toks] = of[rows, :].reshape(B // PIECES, H, of.shape[1]).astype(jnp.bfloat16)
                out_copy(half, k).start()

        def out_copy(half, k):
            toks = pl.ds(half * B + k * B // PIECES, B // PIECES)
            return pltpu.make_async_copy(ob.at[toks], out_h.at[toks], sem_o.at[half * PIECES + k])

        if first:
            counts = [((2 + j) // 2, (2 * ns - j + 1) // 2) for j in range(ns)]
        else:
            counts = [((j + 1) // 2, (2 * ns - j + 1) // 2) for j in range(ns + 1)]
        if len(counts) == 1:
            process((0, counts[0][0], low_l, nl), (1, counts[0][1], high_l, nh))
        elif ns == 4:
            usual = nl == 2
            pl.when(usual)(lambda: process((0, *counts[2][:1], low_l, None), (1, counts[2][1], high_l, None)))
            for half, lst, nb in ((0, low_l, nl), (1, high_l, nh)):
                items = (nb + 1) // 2
                for n in sorted({c[half] for j, c in enumerate(counts) if j != 2}):
                    pl.when((items == n) & (nl != 2))(functools.partial(process, (half, n, lst, nb)))
        else:
            for half, lst, nb in ((0, low_l, nl), (1, high_l, nh)):
                items = (nb + 1) // 2
                for n in sorted({c[half] for c in counts}):
                    pl.when(items == n)(functools.partial(process, (half, n, lst, nb)))
        if last:
            for half in range(2):
                for k in range(PIECES):
                    out_copy(half, k).wait()

    if when is None:
        run()
    else:
        pl.when(when(place_now()))(run)


def phase(first, last, offsets, pos, queries, w_uv, shards, where, when=None, state=None, limit=14):
    ns = len(where)
    T = 256
    B = T // 2
    LATW = shards[0].shape[1]
    packed = shards[0].shape[0]
    R = 2 * (packed - T)
    W = -(-(LATW + R) // 128) * 128
    if first:
        qn, qr, wk = queries
        H = qn.shape[1]
    else:
        H = queries[0].shape[1] // B
    HB = H * B
    vm = pl.BlockSpec(memory_space=pltpu.VMEM)
    hbm = pl.BlockSpec(memory_space=pltpu.HBM)
    bf, f32 = jnp.bfloat16, jnp.float32
    in_specs = [hbm] * 3 if first else [hbm] + [vm] * 4
    keep = lambda xs, space: [pltpu.with_memory_space_constraint(x, space) for x in xs]
    args = keep(queries, pltpu.HBM) if first else [*keep([pos], pltpu.HBM), *keep(queries, pltpu.VMEM)]
    if last:
        in_specs.append(hbm)
        args += keep([w_uv], pltpu.HBM)
    in_specs += [vm] * len(shards)
    args += keep(shards, pltpu.VMEM)
    again = state is not None
    aliases = {}
    if first and not last:
        if again:
            aliases = {len(args) + i: i for i in range(4)}
            in_specs += [vm] * 4
            args += keep(state, pltpu.VMEM)
        else:
            aliases = {}
    q_shape = (2, HB, W)
    if last:
        out_shape = jax.ShapeDtypeStruct((T, H, w_uv.shape[2]), bf)
        out_specs = hbm
        scratch = [pltpu.VMEM(q_shape, bf)] if first else []
    else:
        out_shape = [
            pltpu.VMEM(q_shape, bf),
            pltpu.VMEM((2, HB, B), f32),
            pltpu.VMEM((2, HB, B), f32),
            pltpu.VMEM((2, HB, LATW), f32),
        ]
        if not first:
            out_shape = out_shape[1:]
        elif not again:
            out_shape.append(pltpu.VMEM(shards[0].shape, bf))
        out_specs = [vm] * len(out_shape)
        scratch = []
    scratch += [
        pltpu.VMEM((2 * ns, W, B), bf),
        pltpu.VMEM((2 * ns, B, LATW), bf),
        pltpu.SMEM((16,), jnp.int32),
        pltpu.SMEM((16,), jnp.int32),
    ]
    if not first:
        scratch += [pltpu.SMEM(pos.shape, jnp.int32), pltpu.SemaphoreType.DMA]
    if first:
        scratch += [
            pltpu.VMEM(qn.shape, bf),
            pltpu.VMEM(qr.shape, bf),
            pltpu.VMEM(wk.shape, bf),
            pltpu.VMEM((T * H, qn.shape[2]), f32),
            pltpu.SemaphoreType.DMA((3,)),
        ]
    if last:
        scratch += [
            pltpu.VMEM(w_uv.shape, bf),
            pltpu.VMEM((2, HB, LATW), bf),
            pltpu.VMEM((T * H, w_uv.shape[2]), f32),
            pltpu.VMEM((T, H, w_uv.shape[2]), bf),
            pltpu.SemaphoreType.DMA,
            pltpu.SemaphoreType.DMA((2 * PIECES,)),
        ]
    made = pl.pallas_call(
        functools.partial(phase_kernel, first, last, offsets, where, packed, when, again),
        out_shape=out_shape,
        in_specs=in_specs,
        out_specs=out_specs,
        scratch_shapes=scratch,
        input_output_aliases=aliases,
        compiler_params=pltpu.CompilerParams(vmem_limit_bytes=limit * MIB),
        cost_estimate=pl.CostEstimate(flops=int(FL * ns), bytes_accessed=4 * MIB, transcendentals=MIB),
        name="first" if first else "last" if last else "middle",
    )(*args)
    return made if first or last else [queries[0], *made]


def pack_kernel(c_h, r_h, out, sem):
    rows = c_h.shape[0]
    half = r_h.shape[0] // 2
    piece = rows // 4
    copies = [
        pltpu.make_async_copy(
            c_h.at[pl.ds(k * piece, piece), :], out.at[pl.ds(k * piece, piece), :], sem.at[2 + k]
        )
        for k in range(4)
    ] + [
        pltpu.make_async_copy(r_h.at[pl.ds(0, half), :], out.at[pl.ds(rows, half), pl.ds(0, rows)], sem.at[0]),
        pltpu.make_async_copy(r_h.at[pl.ds(half, half), :], out.at[pl.ds(rows, half), pl.ds(rows, rows)], sem.at[1]),
    ]
    for copy in copies:
        copy.start()
    for copy in copies:
        copy.wait()


def pack(c_kv, k_rope_t):
    rows, width = c_kv.shape
    hbm = pl.BlockSpec(memory_space=pltpu.HBM)
    return pl.pallas_call(
        pack_kernel,
        out_shape=pltpu.VMEM((rows + k_rope_t.shape[0] // 2, width), c_kv.dtype),
        in_specs=[hbm, hbm],
        out_specs=pl.BlockSpec(memory_space=pltpu.VMEM),
        scratch_shapes=[pltpu.SemaphoreType.DMA((6,))],
        compiler_params=pltpu.CompilerParams(vmem_limit_bytes=2 * MIB),
        name="pack",
    )(*[pltpu.with_memory_space_constraint(x, pltpu.HBM) for x in (c_kv, k_rope_t)])


def join_parity_kernel(own, even, odd, _, out):
    rows = own.shape[0]
    out[:rows, :] = own[...]
    parity = lax.rem(place_now(), 2)
    for k, array in enumerate((even, odd)):

        @pl.when(parity == k)
        def _():
            out[rows:, :] = array[...]


def join_parity(after, own, even, odd):
    vm = pl.BlockSpec(memory_space=pltpu.VMEM)
    rows, width = own.shape
    return pl.pallas_call(
        join_parity_kernel,
        out_shape=pltpu.VMEM((2 * rows, width), own.dtype),
        in_specs=[vm] * 4,
        out_specs=vm,
        compiler_params=pltpu.CompilerParams(vmem_limit_bytes=2 * MIB),
        name="join_parity",
    )(*[pltpu.with_memory_space_constraint(x, pltpu.VMEM) for x in (own, even, odd, after)])


def join_kernel(*refs):
    *arrays, _, out = refs
    rows = arrays[0].shape[0]
    for i, array in enumerate(arrays):
        out[i * rows:(i + 1) * rows, :] = array[...]


def join(after, *arrays):
    vm = pl.BlockSpec(memory_space=pltpu.VMEM)
    rows, width = arrays[0].shape
    return pl.pallas_call(
        join_kernel,
        out_shape=pltpu.VMEM((len(arrays) * rows, width), arrays[0].dtype),
        in_specs=[vm] * (1 + len(arrays)),
        out_specs=vm,
        compiler_params=pltpu.CompilerParams(vmem_limit_bytes=2 * MIB),
        name="join",
    )(*[pltpu.with_memory_space_constraint(x, pltpu.VMEM) for x in (*arrays, after)])


def pairs(n, heads, source):
    out = []
    for t in range(n):
        s = source(t)
        if s is None:
            continue
        s %= n
        for h in range(heads):
            hs = h if s // 4 == t // 4 or (s // 16 != t // 16 and not (abs(s - t) > n // 2 and t % 2)) else heads - 1 - h
            out.append((s * heads + hs, t * heads + h))
    return out


def per_device(q_nope, q_rope, c_kv, k_rope, block_pos, w_uk, w_uv):
    n, heads = lax.axis_size("ctx"), lax.axis_size("head")
    send = lambda x, source: lax.ppermute(x, ("ctx", "head"), pairs(n, heads, source))
    mine = pack(c_kv, k_rope.T)
    rows = mine.shape[0]
    queries = (q_nope, jnp.transpose(q_rope, (1, 2, 0)), w_uk)
    side = lambda place: 2 * lax.rem(place, 2) - 1
    near = lambda place: (0,)
    own = [[(0, 0)]]
    below = send(mine, lambda t: t - 2)
    above = send(mine, lambda t: t + 2 if t < n - 4 else None)
    *state, mine = phase(True, False, near, block_pos, queries, w_uv, [mine], own, when=lambda p: p < 2)
    turn = send(mine, lambda t: t + 2 if t >= n - 4 else None)
    state = phase(
        True, False, near, block_pos, queries, w_uv, [mine], own, when=lambda p: p >= 2, state=state
    )
    mate = send(join_parity(state[1], mine, above, below), lambda t: t ^ 1)
    to_end = send(join(state[1], turn), lambda t: t - 1 if t >= n - 4 and t % 2 else None)
    return phase(
        False,
        True,
        lambda p: (side(p), 2, -2, -side(p)),
        block_pos,
        state,
        w_uv,
        [below, above, turn, mate, to_end],
        [[(3, 0)], [(0, 0)], [(1, 0), (2, 0)], [(3, rows), (4, 0)]],
    )


def solution(mesh):
    placed = (
        P("ctx", "head", None),
        P("ctx", "head", None),
        P("ctx", None),
        P("ctx", None),
        P(),
        P("head", None, None),
        P("head", None, None),
    )
    return jax.shard_map(
        per_device, mesh=mesh, in_specs=placed, out_specs=P("ctx", "head", None), check_vma=False
    )
```
